256 devices in a mesh: band: 64 (over z, y, core), col: 4 (over x).
Axes of the slice: x: 4, y: 4, z: 8, core: 2. Of those that a mesh axis runs over, the one named last changes fastest.
Arguments:
- prior_basis: float32 [64, 2, 4, 512, 1024], P(None, None, None, 'band', 'col'), may hold values from -0.0043945312 to 0.0043945312, as said below
- coupling: float32 [2, 4, 4, 512, 1024], P(None, None, None, 'band', 'col'), may hold values from -1.8 to 1.8
- velocity: float32 [2, 512, 1024], P(None, 'band', 'col'), may hold values from -0.5 to 1
Outputs:
- basis_next: float32 [64, 2, 4, 512, 1024], P(None, None, None, 'band', 'col')
- triangle: float32 [64, 64], replicated
The draws below stay inside these ranges and needn't reach their ends.
Inputs may be any that keep to these rules, and one draw needn't show every extreme that they name: `prior_basis`: 64 earlier basis vectors.
All inputs are finite; a program needn't handle non-finite values.
Results may differ from the reference program's by a relative error of at most 0.0013.
Values sent between devices are 32-bit elements; how exact they have to be, the bound alone decides.
No kernel may reach another device: no remote copies, remote signals or barrier semaphores. Data moves between devices by JAX's collectives and lax.ppermute only.
A program may use at most 64 MiB of HBM per device.

```python
import math
import jax
import jax.numpy as jnp
from jax import lax

FIELDS = 4
BLOCK = 16
STEPS = 4
KPREV = 64
NROWS = 512
NCOLS = 1024


def base_coupling(key):
    key = jax.random.fold_in(key, 101)
    values = jax.random.truncated_normal(key, -6.0, 6.0, (2, FIELDS, FIELDS, NROWS, NCOLS), jnp.float32)
    return 0.3 * values


def base_velocity(key):
    key = jax.random.fold_in(key, 202)
    return jax.random.uniform(key, (2, NROWS, NCOLS), jnp.float32, -0.5, 1.0)


def krylov_step(vector, coupling, velocity):
    padded = jnp.pad(vector, ((0, 0), (0, 0), (1, 1), (1, 1)))
    center = padded[:, :, 1:-1, 1:-1]
    upper_row = padded[:, :, 2:, 1:-1]
    lower_row = padded[:, :, :-2, 1:-1]
    right_col = padded[:, :, 1:-1, 2:]
    left_col = padded[:, :, 1:-1, :-2]
    spread = 0.15 * (upper_row + lower_row + right_col + left_col - 4.0 * center)
    carried = 0.5 * velocity[0] * (upper_row - lower_row) + 0.5 * velocity[1] * (right_col - left_col)
    mixing_real = jnp.zeros_like(center[0])
    mixing_imag = jnp.zeros_like(center[1])
    for source in range(FIELDS):
        coeff_real = coupling[0][:, source]
        coeff_imag = coupling[1][:, source]
        real_src = center[0][source][None]
        imag_src = center[1][source][None]
        mixing_real = mixing_real + coeff_real * real_src - coeff_imag * imag_src
        mixing_imag = mixing_imag + coeff_real * imag_src + coeff_imag * real_src
    return spread - carried + jnp.stack([mixing_real, mixing_imag], axis=0)


def draw_coupling(key, part):
    shared = base_coupling(key)
    return shared


def draw_velocity(key, part):
    shared = base_velocity(key)
    return shared


def draw_prior_basis(key, part):
    coupling = base_coupling(key)
    velocity = base_velocity(key)
    key = jax.random.fold_in(key, 17)
    values_key, scale_key = jax.random.split(key)
    seed_shape = (BLOCK, 2, FIELDS, NROWS, NCOLS)
    row_rise = jnp.exp(jnp.log(3.0) * jnp.arange(NROWS, dtype=jnp.float32) / NROWS)
    roughness = jax.random.uniform(scale_key, (NROWS, NCOLS), jnp.float32, 0.5, 1.5)
    amplitude = row_rise[:, None] * roughness
    values = jax.random.truncated_normal(values_key, -4.0, 4.0, seed_shape, jnp.float32)
    amplitude = amplitude / 2.0
    current = values * amplitude * (8.0 * NROWS * NCOLS) ** (-0.5)
    gathered = [current]
    for depth_idx in range(1, KPREV // BLOCK):
        current = lax.map(lambda vector: krylov_step(vector, coupling, velocity), current) / 1.2
        gathered.append(current)
    clip_bound = 9.0 * (8.0 * NROWS * NCOLS) ** (-0.5)
    return jnp.clip(jnp.concatenate(gathered, axis=0), -clip_bound, clip_bound)


def setup_inputs(seed: int = 0) -> dict:
    arg_keys = jax.random.split(jax.random.key(seed), 4)
    return {
        "prior_basis": draw_prior_basis(jax.random.fold_in(arg_keys[3], 71), 0),
        "coupling": draw_coupling(jax.random.fold_in(arg_keys[3], 71), 0),
        "velocity": draw_velocity(jax.random.fold_in(arg_keys[3], 71), 0),
    }


def apply_operator(padded, coupling, velocity):
    center = padded[..., 1:-1, 1:-1]
    upper_row = padded[..., 2:, 1:-1]
    lower_row = padded[..., :-2, 1:-1]
    right_col = padded[..., 1:-1, 2:]
    left_col = padded[..., 1:-1, :-2]
    spread = 0.15 * (upper_row + lower_row + right_col + left_col - 4.0 * center)
    carried = 0.5 * velocity[0] * (upper_row - lower_row) + 0.5 * velocity[1] * (right_col - left_col)
    real_part = center[:, 0]
    imag_part = center[:, 1]
    mixing_real = jnp.zeros_like(real_part)
    mixing_imag = jnp.zeros_like(imag_part)
    for source in range(real_part.shape[1]):
        coeff_real = coupling[0][:, source][None]
        coeff_imag = coupling[1][:, source][None]
        real_src = real_part[:, source][:, None]
        imag_src = imag_part[:, source][:, None]
        mixing_real = mixing_real + coeff_real * real_src - coeff_imag * imag_src
        mixing_imag = mixing_imag + coeff_real * imag_src + coeff_imag * real_src
    mixing = jnp.stack([mixing_real, mixing_imag], axis=1)
    return spread - carried + mixing

def reference(prior_basis, coupling, velocity):
    highest = lax.Precision.HIGHEST
    current = prior_basis[KPREV - BLOCK:]
    powers = []
    for power_idx in range(STEPS):
        padded = jnp.pad(current, ((0, 0), (0, 0), (0, 0), (1, 1), (1, 1)))
        current = apply_operator(padded, coupling, velocity)
        powers.append(current)
    stacked = jnp.concatenate(powers, axis=0)
    new_count = stacked.shape[0]
    flat_basis = prior_basis.reshape(KPREV, -1)
    flat_powers = stacked.reshape(new_count, -1)
    coeffs = jnp.dot(flat_basis, flat_powers.T, precision=highest)
    projected = flat_powers - jnp.dot(coeffs.T, flat_basis, precision=highest)
    gram_matrix = jnp.dot(projected, projected.T, precision=highest)
    lower_factor = jnp.linalg.cholesky(gram_matrix)
    solved = jax.scipy.linalg.solve_triangular(lower_factor, projected, lower=True)
    unknowns = 2 * FIELDS * NROWS * NCOLS
    basis_next = (solved * math.sqrt(unknowns)).reshape(stacked.shape)
    return (basis_next, lower_factor.T)
```

```python
import math

import jax
import jax.numpy as jnp
from jax import lax
from jax.experimental import pallas as pl
from jax.experimental.pallas import tpu as pltpu
from jax.sharding import PartitionSpec as P

BLOCK = 16
STEPS = 4
KPREV = 64
COMPS = 8
ROWS = 8
COLS = 256
LANES = 128
WIDTH = 4
PLANES = COMPS * BLOCK
COUPLINGS = 32
COEFFS = 40
SLAB = PLANES + COEFFS
TILES = SLAB // 8
PACKED = (TILES + 1) // 2
SPAN = ROWS + 2 * WIDTH
WIDE = COLS + LANES
BOTH = 2 * KPREV

ANY = pl.BlockSpec(memory_space=pl.ANY)
VMEM = pl.BlockSpec(memory_space=pltpu.VMEM)


def core_of_chip():
    return lax.rem(lax.axis_index("band"), 2)


def pack_kernel(basis, coupling, velocity, slab_out, core_out, chip_out, edges, slab, sems, out_sems):
    copies = []
    for row in range(ROWS):
        for comp in range(COMPS):
            copies.append(
                pltpu.make_async_copy(
                    basis.at[pl.ds(KPREV - BLOCK, BLOCK), comp, row, :],
                    slab.at[row, pl.ds(comp * BLOCK, BLOCK), :],
                    sems.at[row, comp],
                )
            )
        copies.append(
            pltpu.make_async_copy(
                coupling.at[:, row, :],
                slab.at[row, pl.ds(PLANES, COUPLINGS), :],
                sems.at[row, COMPS],
            )
        )
    for copy in copies:
        copy.start()
    half_rows = 0.5 * velocity[0]
    half_cols = 0.5 * velocity[1]
    stencil = (0.15 - half_rows, 0.15 + half_rows, 0.15 - half_cols, 0.15 + half_cols)
    blank = jnp.zeros((4, COLS), jnp.float32)
    for row in range(ROWS):
        slab[row, PLANES + COUPLINGS :, :] = jnp.concatenate(
            [part[row : row + 1] for part in stencil] + [blank], axis=0
        )
    for copy in copies:
        copy.wait()
    core = core_of_chip()
    inner = pl.multiple_of((1 - core) * WIDTH, WIDTH)
    outer = pl.multiple_of(core * WIDTH, WIDTH)
    outs = [
        pltpu.make_async_copy(slab.at[pl.ds(inner, WIDTH)], core_out, out_sems.at[0]),
        pltpu.make_async_copy(slab.at[pl.ds(outer, WIDTH)], chip_out, out_sems.at[1]),
        pltpu.make_async_copy(slab, slab_out, out_sems.at[2]),
    ]
    for copy in outs:
        copy.start()
    lane = lax.broadcasted_iota(jnp.int32, (8, LANES), 1)
    for packed in range(PACKED):
        total = jnp.zeros((8, LANES), jnp.float32)
        for half in range(2):
            tile = 2 * packed + half
            if tile >= TILES:
                continue
            for row in range(ROWS):
                group = half * ROWS + row
                first = slab[row, tile * 8 : tile * 8 + 8, 0:LANES]
                last = slab[row, tile * 8 : tile * 8 + 8, COLS - LANES : COLS]
                edge = pltpu.roll(jnp.where(lane < WIDTH, first, last), (8 * group + 4) % LANES, 1)
                total = jnp.where(lane // 8 == group, edge, total)
        edges[packed] = total
    for copy in outs:
        copy.wait()


def operator_row(cur, nxt, coef, row, tiles):
    width = tiles * LANES

    def coeff(plane):
        return jnp.broadcast_to(coef[row, pl.ds(plane, 1), 0:width], (BLOCK, width))

    lower_c, upper_c = coeff(COUPLINGS + 1), coeff(COUPLINGS)
    right_c, left_c = coeff(COUPLINGS + 2), coeff(COUPLINGS + 3)
    center = []
    sums = []
    for comp in range(COMPS):
        planes = pl.ds(comp * BLOCK, BLOCK)
        here = cur[row, planes, :]
        right = pltpu.roll(here, WIDE - 1, 1)[:, :width]
        left = pltpu.roll(here, 1, 1)[:, :width]
        center.append(here[:, :width])
        sums.append(
            upper_c * cur[row + 1, planes, 0:width]
            + lower_c * cur[row - 1, planes, 0:width]
            + right_c * right
            + left_c * left
        )
    for field in range(4):
        real, imag = sums[field], sums[4 + field]
        for source in range(4):
            coeff_real = coeff(field * 4 + source)
            coeff_imag = coeff(16 + field * 4 + source)
            if source == field:
                coeff_real = coeff_real - 0.6
            real = real + coeff_real * center[source] - coeff_imag * center[4 + source]
            imag = imag + coeff_real * center[4 + source] + coeff_imag * center[source]
        nxt[row, pl.ds(field * BLOCK, BLOCK), 0:width] = real
        nxt[row, pl.ds((4 + field) * BLOCK, BLOCK), 0:width] = imag


def split(value):
    high = value.astype(jnp.bfloat16)
    return high, (value - high.astype(jnp.float32)).astype(jnp.bfloat16)


def power_kernel(
    basis, slab, from_core, from_chip, sides, core_sides, chip_sides,
    split_out, inner_out,
    ping, pong, coef, prior, parts, total, sems, halo_sems, out_sems,
):
    core = core_of_chip()
    is_first = core == 0
    core_at = pl.multiple_of((1 - core) * (SPAN - WIDTH), WIDTH)
    chip_at = pl.multiple_of(core * (SPAN - WIDTH), WIDTH)
    halos = []
    for index, (source, where, count) in enumerate(
        ((slab, WIDTH, ROWS), (from_core, core_at, WIDTH), (from_chip, chip_at, WIDTH))
    ):
        halos.append(
            pltpu.make_async_copy(
                source.at[:, pl.ds(0, PLANES), :],
                ping.at[pl.ds(where, count), :, pl.ds(0, COLS)],
                halo_sems.at[2 * index],
            )
        )
        halos.append(
            pltpu.make_async_copy(
                source.at[:, pl.ds(PLANES, COEFFS), :],
                coef.at[pl.ds(where, count), :, pl.ds(0, COLS)],
                halo_sems.at[2 * index + 1],
            )
        )
    for copy in halos:
        copy.start()
    copies = []
    for row in range(ROWS):
        for comp in range(COMPS):
            copies.append(
                pltpu.make_async_copy(
                    basis.at[:, comp, row, :],
                    prior.at[row, :, pl.ds(comp * COLS, COLS)],
                    sems.at[row, comp],
                )
            )
    for copy in copies:
        copy.start()
    lane = lax.broadcasted_iota(jnp.int32, (8, LANES), 1)
    near = (lane < WIDTH) | (lane >= LANES - WIDTH)
    for packed in range(PACKED):
        own = sides[packed]
        by_core, by_chip = core_sides[packed], chip_sides[packed]
        above = jnp.where(is_first, by_core, by_chip)
        below = jnp.where(is_first, by_chip, by_core)
        for half in range(2):
            tile = 2 * packed + half
            if tile >= TILES:
                continue
            for row in range(SPAN):
                if row < WIDTH:
                    source, source_row = below, row + ROWS - WIDTH
                elif row < WIDTH + ROWS:
                    source, source_row = own, row - WIDTH
                else:
                    source, source_row = above, row - WIDTH - ROWS
                group = half * ROWS + source_row
                edge = pltpu.roll(source, (2 * LANES - 8 * group - 4) % LANES, 1)
                edge = jnp.where(near, edge, 0.0)
                if tile < PLANES // 8:
                    ping[row, tile * 8 : tile * 8 + 8, COLS:WIDE] = edge
                else:
                    at = tile * 8 - PLANES
                    coef[row, at : at + 8, COLS:WIDE] = edge
    for copy in halos:
        copy.wait()
    buffers = (ping, pong)
    for step in range(1, STEPS + 1):
        cur, nxt = buffers[(step - 1) % 2], buffers[step % 2]
        tiles = 3 if step < STEPS else 2

        def one_row(row, carry, cur=cur, nxt=nxt, tiles=tiles):
            for tile in range(1):
                operator_row(cur, nxt, coef, row, tiles)
            return carry

        lax.fori_loop(step, SPAN - step, one_row, 0)

        def one_split(row, carry, nxt=nxt, step=step):
            at = KPREV + (step - 1) * BLOCK
            for comp in range(COMPS):
                high, low = split(nxt[row + WIDTH, pl.ds(comp * BLOCK, BLOCK), 0:COLS])
                parts[row, pl.ds(at, BLOCK), pl.ds(comp * COLS, COLS)] = high
                parts[row, pl.ds(BOTH + at, BLOCK), pl.ds(comp * COLS, COLS)] = low
            return carry

        lax.fori_loop(0, ROWS, one_split, 0)
    for copy in copies:
        copy.wait()

    def split_prior(row, carry):
        for at in range(0, KPREV, BLOCK):
            high, low = split(prior[row, pl.ds(at, BLOCK), :])
            parts[row, pl.ds(at, BLOCK), :] = high
            parts[row, pl.ds(BOTH + at, BLOCK), :] = low
        return carry

    lax.fori_loop(0, ROWS, split_prior, 0)
    outs = [
        pltpu.make_async_copy(parts.at[row], split_out.at[row], out_sems.at[row]) for row in range(ROWS)
    ]
    for copy in outs:
        copy.start()
    total[...] = jnp.zeros_like(total)

    def products(row, carry):
        block = parts[row]
        total[...] += lax.dot_general(
            block, block, (((1,), (1,)), ((), ())), preferred_element_type=jnp.float32
        )
        return carry

    lax.fori_loop(0, ROWS, products, 0)
    inner = (
        total[0:BOTH, 0:BOTH] + (total[BOTH:, 0:BOTH] + total[0:BOTH, BOTH:]) + total[BOTH:, BOTH:]
    )
    inner_out[0:KPREV] = inner[0:KPREV]
    new = inner[KPREV:, KPREV:]
    inner_out[KPREV:] = jnp.concatenate([new[: KPREV // 2], new[KPREV // 2 :]], axis=1)
    for copy in outs:
        copy.wait()


def finish_kernel(inner, split_in, basis_out, triangle_out, parts, result, in_sems, out_sems):
    loads = [
        pltpu.make_async_copy(split_in.at[row], parts.at[row], in_sems.at[row]) for row in range(ROWS)
    ]
    for copy in loads:
        copy.start()

    def dot(a, b, dims):
        return lax.dot_general(
            a, b, (dims, ((), ())), precision=lax.Precision.HIGHEST, preferred_element_type=jnp.float32
        )

    prior = inner[0:KPREV, 0:KPREV]
    coeffs = inner[0:KPREV, KPREV:]
    half = KPREV // 2
    new = jnp.concatenate([inner[KPREV:, 0:KPREV], inner[KPREV:, KPREV:]], axis=0)
    mixed = dot(prior, coeffs, ((1,), (0,))) - 2.0 * coeffs
    gram = new + dot(coeffs, mixed, ((0,), (0,)))
    del half
    row_id = lax.broadcasted_iota(jnp.int32, (KPREV, 2 * KPREV), 0)
    col_id = lax.broadcasted_iota(jnp.int32, (KPREV, 2 * KPREV), 1)
    unit = jnp.where(
        lax.broadcasted_iota(jnp.int32, (KPREV, KPREV), 0)
        == lax.broadcasted_iota(jnp.int32, (KPREV, KPREV), 1),
        1.0,
        0.0,
    )
    work = jnp.concatenate([gram, unit], axis=1)
    for pivot in range(KPREV - 1):
        row = work[pivot : pivot + 1, :]
        scaled = row * (1.0 / row[:, pivot : pivot + 1])
        column = work[:, pivot : pivot + 1]
        work = jnp.where(row_id > pivot, work - column * scaled, work)
    diagonal = jnp.sum(jnp.where(row_id == col_id, work, 0.0), axis=1, keepdims=True)
    work = work / jnp.sqrt(diagonal)
    upper = work[:, :KPREV]
    triangle_out[...] = jnp.where(col_id[:, :KPREV] >= row_id[:, :KPREV], upper, 0.0)
    unknowns = 2 * 4 * 512 * 1024
    inverse = work[:, KPREV:] * math.sqrt(unknowns)
    weights = jnp.concatenate([-dot(inverse, coeffs, ((1,), (1,))), inverse], axis=1)
    high, low = split(weights)
    left = jnp.concatenate(
        [
            jnp.concatenate([high, high], axis=1),
            jnp.concatenate([low, jnp.zeros_like(low)], axis=1),
        ],
        axis=0,
    )
    stores = []
    for row in range(ROWS):
        loads[row].wait()
        for comp in range(COMPS):
            both = jnp.dot(
                left, parts[row, :, comp * COLS : (comp + 1) * COLS], preferred_element_type=jnp.float32
            )
            result[row, comp] = both[:KPREV] + both[KPREV:]
            copy = pltpu.make_async_copy(
                result.at[row, comp], basis_out.at[:, comp, row, :], out_sems.at[row, comp]
            )
            copy.start()
            stores.append(copy)
    for copy in stores:
        copy.wait()


def pairs_in(size, partner):
    return [(i, partner(i)) for i in range(size) if partner(i) is not None]


def row_exchange(value, bands, across):
    def partner(i):
        j = i + (1 if (i % 2 == 0) == (not across) else -1)
        return j if 0 <= j < bands else None

    return lax.ppermute(value, "band", pairs_in(bands, partner))


def col_exchange(value, cols, odd):
    def partner(i):
        j = i + (1 if (i % 2 == 0) == (not odd) else -1)
        return j if 0 <= j < cols else None

    return lax.ppermute(value, "col", pairs_in(cols, partner))


def sum_over_devices(value, bands, cols):
    def swap(part, mask):
        bits = cols - 1
        col_mask, band_mask = mask & bits, mask // cols
        perm = [(i, i ^ mask) for i in range(bands * cols)]
        del col_mask, band_mask
        return lax.ppermute(part, ("band", "col"), perm)

    mask = 1
    masks = []
    while mask < bands * cols:
        masks.append(mask)
        mask *= 2
    masks.sort(key=lambda m: (m != cols, m))
    for mask in masks:
        value = value + swap(value, mask)
    return value


def per_device(prior_basis, coupling, velocity):
    bands, cols = lax.axis_size("band"), lax.axis_size("col")
    f32 = jnp.float32
    basis = prior_basis.reshape(KPREV, COMPS, ROWS, COLS)
    slab, to_core, to_chip, edges = pl.pallas_call(
        pack_kernel,
        out_shape=(
            jax.ShapeDtypeStruct((ROWS, SLAB, COLS), f32),
            jax.ShapeDtypeStruct((WIDTH, SLAB, COLS), f32),
            jax.ShapeDtypeStruct((WIDTH, SLAB, COLS), f32),
            jax.ShapeDtypeStruct((PACKED, 8, LANES), f32),
        ),
        in_specs=[ANY, ANY, VMEM],
        out_specs=(ANY, ANY, ANY, VMEM),
        scratch_shapes=[
            pltpu.VMEM((ROWS, SLAB, COLS), f32),
            pltpu.SemaphoreType.DMA((ROWS, COMPS + 1)),
            pltpu.SemaphoreType.DMA((3,)),
        ],
        name="pack",
    )(basis, coupling.reshape(COUPLINGS, ROWS, COLS), velocity)
    side_even = col_exchange(edges, cols, False)
    side_odd = col_exchange(edges, cols, True)
    from_core = row_exchange(to_core, bands, False)
    from_chip = row_exchange(to_chip, bands, True)
    col_is_even = lax.rem(lax.axis_index("col"), 2) == 0
    from_right = lax.broadcasted_iota(jnp.int32, edges.shape, 2) % 8 >= 4
    sides = jnp.where(from_right == col_is_even, side_even, side_odd)
    core_sides = row_exchange(sides, bands, False)
    chip_sides = row_exchange(sides, bands, True)
    parts, inner = pl.pallas_call(
        power_kernel,
        out_shape=(
            jax.ShapeDtypeStruct((ROWS, 2 * BOTH, COMPS * COLS), jnp.bfloat16),
            jax.ShapeDtypeStruct((KPREV + KPREV // 2, BOTH), f32),
        ),
        in_specs=[ANY, ANY, ANY, ANY, VMEM, VMEM, VMEM],
        out_specs=(ANY, VMEM),
        scratch_shapes=[
            pltpu.VMEM((SPAN, PLANES, WIDE), f32),
            pltpu.VMEM((SPAN, PLANES, WIDE), f32),
            pltpu.VMEM((SPAN, COEFFS, WIDE), f32),
            pltpu.VMEM((ROWS, KPREV, COMPS * COLS), f32),
            pltpu.VMEM((ROWS, 2 * BOTH, COMPS * COLS), jnp.bfloat16),
            pltpu.VMEM((2 * BOTH, 2 * BOTH), f32),
            pltpu.SemaphoreType.DMA((ROWS, COMPS)),
            pltpu.SemaphoreType.DMA((6,)),
            pltpu.SemaphoreType.DMA((ROWS,)),
        ],
        compiler_params=pltpu.CompilerParams(vmem_limit_bytes=48 * 1024 * 1024),
        name="powers",
    )(basis, slab, from_core, from_chip, sides, core_sides, chip_sides)
    inner = sum_over_devices(inner, bands, cols)
    basis_next, triangle = pl.pallas_call(
        finish_kernel,
        out_shape=(
            jax.ShapeDtypeStruct((KPREV, COMPS, ROWS, COLS), f32),
            jax.ShapeDtypeStruct((KPREV, KPREV), f32),
        ),
        in_specs=[VMEM, ANY],
        out_specs=(ANY, VMEM),
        scratch_shapes=[
            pltpu.VMEM((ROWS, 2 * BOTH, COMPS * COLS), jnp.bfloat16),
            pltpu.VMEM((ROWS, COMPS, KPREV, COLS), f32),
            pltpu.SemaphoreType.DMA((ROWS,)),
            pltpu.SemaphoreType.DMA((ROWS, COMPS)),
        ],
        compiler_params=pltpu.CompilerParams(vmem_limit_bytes=48 * 1024 * 1024),
        name="finish",
    )(inner, parts)
    return (basis_next.reshape(prior_basis.shape), triangle)


def solution(mesh):
    in_specs = (
        P(None, None, None, "band", "col"),
        P(None, None, None, "band", "col"),
        P(None, "band", "col"),
    )
    out_specs = (P(None, None, None, "band", "col"), P())
    return jax.shard_map(
        per_device, mesh=mesh, in_specs=in_specs, out_specs=out_specs, check_vma=False
    )
```

```python
import math

import jax
import jax.numpy as jnp
from jax import lax
from jax.experimental import pallas as pl
from jax.experimental.pallas import tpu as pltpu
from jax.sharding import PartitionSpec as P

BLOCK = 16
STEPS = 4
KPREV = 64
COMPS = 8
ROWS = 8
COLS = 256
LANES = 128
WIDTH = 4
PLANES = COMPS * BLOCK
COUPLINGS = 32
COEFFS = 40
SLAB = PLANES + COEFFS
TILES = SLAB // 8
PACKED = (TILES + 1) // 2
SPAN = ROWS + 2 * WIDTH
WIDE = COLS + LANES
BOTH = 2 * KPREV
PIVOTS = 8
CELL_ROWS = COMPS * ROWS
OUT = pltpu.VMEM

ANY = pl.BlockSpec(memory_space=pl.ANY)
VMEM = pl.BlockSpec(memory_space=pltpu.VMEM)
HBM = pl.BlockSpec(memory_space=pltpu.HBM)


def core_of_chip():
    return lax.rem(lax.axis_index("band"), 2)


def pack_kernel(basis, coupling, velocity, slab, core_out, chip_out, edges, start, mixing, sems):
    loads = []
    for half in range(2):
        lanes = pl.ds(half * LANES, LANES)
        loads += [
            pltpu.make_async_copy(
                basis.at[pl.ds((KPREV - BLOCK) * CELL_ROWS, BLOCK * CELL_ROWS), lanes],
                start.at[half],
                sems.at[half],
            ),
            pltpu.make_async_copy(coupling.at[:, lanes], mixing.at[half], sems.at[2 + half]),
        ]
    for copy in loads:
        copy.start()
    half_rows = 0.5 * velocity[0]
    half_cols = 0.5 * velocity[1]
    stencil = (0.15 - half_rows, 0.15 + half_rows, 0.15 - half_cols, 0.15 + half_cols)
    blank = jnp.zeros((4, COLS), jnp.float32)
    for row in range(ROWS):
        slab[row, PLANES + COUPLINGS :, :] = jnp.concatenate(
            [part[row : row + 1] for part in stencil] + [blank], axis=0
        )
    for copy in loads:
        copy.wait()
    for row in range(ROWS):
        for half in range(2):
            lanes = slice(half * LANES, (half + 1) * LANES)
            for comp in range(COMPS):
                slab[row, comp * BLOCK : (comp + 1) * BLOCK, lanes] = start[
                    half, pl.ds(comp * ROWS + row, BLOCK, stride=CELL_ROWS), :
                ]
            slab[row, PLANES : PLANES + COUPLINGS, lanes] = mixing[
                half, pl.ds(row, COUPLINGS, stride=ROWS), :
            ]
    core = core_of_chip()
    for row in range(WIDTH):
        core_out[row] = slab[row + (1 - core) * WIDTH]
        chip_out[row] = slab[row + core * WIDTH]
    lane = lax.broadcasted_iota(jnp.int32, (8, LANES), 1)
    for packed in range(PACKED):
        total = jnp.zeros((8, LANES), jnp.float32)
        for half in range(2):
            tile = 2 * packed + half
            if tile >= TILES:
                continue
            for row in range(ROWS):
                group = half * ROWS + row
                first = slab[row, tile * 8 : tile * 8 + 8, 0:LANES]
                last = slab[row, tile * 8 : tile * 8 + 8, COLS - LANES : COLS]
                edge = pltpu.roll(jnp.where(lane < WIDTH, first, last), (8 * group + 4) % LANES, 1)
                total = jnp.where(lane // 8 == group, edge, total)
        edges[packed] = total


def split(value):
    high = value.astype(jnp.bfloat16)
    return high, (value - high.astype(jnp.float32)).astype(jnp.bfloat16)


def prior_kernel(basis, parts, token, native, sems):
    pieces = KPREV // BLOCK
    size = BLOCK * CELL_ROWS
    loads = [
        pltpu.make_async_copy(
            basis.at[pl.ds(piece * size, size), pl.ds(half * LANES, LANES)],
            native.at[half, pl.ds(piece * size, size), :],
            sems.at[piece, half],
        )
        for piece in range(pieces)
        for half in range(2)
    ]
    for copy in loads:
        copy.start()
    for piece in range(pieces):
        loads[2 * piece].wait()
        loads[2 * piece + 1].wait()

        def one_row(row, carry, piece=piece):
            for comp in range(COMPS):
                for half in range(2):
                    at = piece * size + comp * ROWS
                    high, low = split(native[half, pl.ds(at + row, BLOCK, stride=CELL_ROWS), :])
                    cells = pl.ds(comp * COLS + half * LANES, LANES)
                    parts[row, pl.ds(piece * BLOCK, BLOCK), cells] = high
                    parts[row, pl.ds(KPREV + piece * BLOCK, BLOCK), cells] = low
            return carry

        lax.fori_loop(0, ROWS, one_row, 0)
    token[...] = jnp.zeros_like(token)


def merge_kernel(side_even, side_odd, after, sides):
    del after
    col_is_even = lax.rem(lax.axis_index("col"), 2) == 0
    from_right = lax.broadcasted_iota(jnp.int32, side_even.shape, 2) % 8 >= 4
    sides[...] = jnp.where(from_right == col_is_even, side_even[...], side_odd[...])


def dot_rows(a, b):
    return lax.dot_general(a, b, (((1,), (1,)), ((), ())), preferred_element_type=jnp.float32)


def join_parts(total):
    crossed = total[KPREV:, 0:KPREV] + total[0:KPREV, KPREV:]
    return total[0:KPREV, 0:KPREV] + crossed + total[KPREV:, KPREV:]


def operator_row(cur, nxt, coef, row, tiles):
    lane = lax.broadcasted_iota(jnp.int32, (BLOCK, LANES), 1)
    is_first, is_last = lane == 0, lane == LANES - 1
    for tile in range(tiles):
        lanes, after, before = (
            pl.ds((tile + shift) % (WIDE // LANES) * LANES, LANES) for shift in (0, 1, WIDE // LANES - 1)
        )

        def coeff(plane, lanes=lanes):
            return jnp.broadcast_to(coef[row, pl.ds(plane, 1), lanes], (BLOCK, LANES))

        def neighbours(comp, here, lanes=lanes, after=after, before=before, coeff=coeff):
            planes = pl.ds(comp * BLOCK, BLOCK)
            right = pltpu.roll(jnp.where(is_first, cur[row, planes, after], here), LANES - 1, 1)
            left = pltpu.roll(jnp.where(is_last, cur[row, planes, before], here), 1, 1)
            return (
                coeff(COUPLINGS) * cur[row + 1, planes, lanes]
                + coeff(COUPLINGS + 1) * cur[row - 1, planes, lanes]
                + coeff(COUPLINGS + 2) * right
                + coeff(COUPLINGS + 3) * left
            )

        center = [cur[row, pl.ds(comp * BLOCK, BLOCK), lanes] for comp in range(COMPS)]
        for field in range(4):
            real = neighbours(field, center[field])
            imag = neighbours(4 + field, center[4 + field])
            for source in range(4):
                coeff_real = coeff(field * 4 + source)
                coeff_imag = coeff(16 + field * 4 + source)
                if source == field:
                    coeff_real = coeff_real - 0.6
                real = real + coeff_real * center[source] - coeff_imag * center[4 + source]
                imag = imag + coeff_real * center[4 + source] + coeff_imag * center[source]
            nxt[row, pl.ds(field * BLOCK, BLOCK), lanes] = real
            nxt[row, pl.ds((4 + field) * BLOCK, BLOCK), lanes] = imag


def power_kernel(
    slab, from_core, from_chip, sides, core_sides, chip_sides, prior_parts,
    parts, inner_out,
    ping, pong, coef, halo_sems,
):
    core = core_of_chip()
    is_first = core == 0
    core_at = pl.multiple_of((1 - core) * (SPAN - WIDTH), WIDTH)
    chip_at = pl.multiple_of(core * (SPAN - WIDTH), WIDTH)
    halos = []
    for index, (source, where, count) in enumerate(
        ((slab, WIDTH, ROWS), (from_core, core_at, WIDTH), (from_chip, chip_at, WIDTH))
    ):
        halos.append(
            pltpu.make_async_copy(
                source.at[:, pl.ds(0, PLANES), :],
                ping.at[pl.ds(where, count), :, pl.ds(0, COLS)],
                halo_sems.at[2 * index],
            )
        )
        halos.append(
            pltpu.make_async_copy(
                source.at[:, pl.ds(PLANES, COEFFS), :],
                coef.at[pl.ds(where, count), :, pl.ds(0, COLS)],
                halo_sems.at[2 * index + 1],
            )
        )
    for copy in halos:
        copy.start()
    lane = lax.broadcasted_iota(jnp.int32, (8, LANES), 1)
    near = (lane < WIDTH) | (lane >= LANES - WIDTH)
    for packed in range(PACKED):
        own = sides[packed]
        by_core, by_chip = core_sides[packed], chip_sides[packed]
        above = jnp.where(is_first, by_core, by_chip)
        below = jnp.where(is_first, by_chip, by_core)
        for half in range(2):
            tile = 2 * packed + half
            if tile >= TILES:
                continue
            for row in range(SPAN):
                if row < WIDTH:
                    source, source_row = below, row + ROWS - WIDTH
                elif row < WIDTH + ROWS:
                    source, source_row = own, row - WIDTH
                else:
                    source, source_row = above, row - WIDTH - ROWS
                group = half * ROWS + source_row
                edge = pltpu.roll(source, (2 * LANES - 8 * group - 4) % LANES, 1)
                edge = jnp.where(near, edge, 0.0)
                if tile < PLANES // 8:
                    ping[row, tile * 8 : tile * 8 + 8, COLS:WIDE] = edge
                else:
                    at = tile * 8 - PLANES
                    coef[row, at : at + 8, COLS:WIDE] = edge
    for copy in halos:
        copy.wait()
    buffers = (ping, pong)
    for step in range(1, STEPS + 1):
        cur, nxt = buffers[(step - 1) % 2], buffers[step % 2]
        tiles = 3 if step < STEPS else 2

        def one_row(row, carry, cur=cur, nxt=nxt, tiles=tiles):
            operator_row(cur, nxt, coef, row, tiles)
            return carry

        lax.fori_loop(step, SPAN - step, one_row, 0)

        def one_split(row, carry, nxt=nxt, step=step):
            at = (step - 1) * BLOCK
            for comp in range(COMPS):
                high, low = split(nxt[row + WIDTH, pl.ds(comp * BLOCK, BLOCK), 0:COLS])
                parts[row, pl.ds(at, BLOCK), pl.ds(comp * COLS, COLS)] = high
                parts[row, pl.ds(KPREV + at, BLOCK), pl.ds(comp * COLS, COLS)] = low
            return carry

        lax.fori_loop(0, ROWS, one_split, 0)
    total = 0.0
    for row in range(ROWS):
        block = jnp.concatenate([prior_parts[row], parts[row]], axis=0)
        total = total + dot_rows(block, block)
    inner_out[0:KPREV] = jnp.concatenate(
        [join_parts(total[:BOTH, :BOTH]), join_parts(total[:BOTH, BOTH:])], axis=1
    )
    new = join_parts(total[BOTH:, BOTH:])
    inner_out[KPREV:] = jnp.concatenate([new[: KPREV // 2], new[KPREV // 2 :]], axis=1)


def finish_kernel(inner, prior_parts, new_parts, basis_out, triangle_out, result, out_sems):
    def dot(a, b, dims):
        return lax.dot_general(
            a, b, (dims, ((), ())), precision=lax.Precision.HIGHEST, preferred_element_type=jnp.float32
        )

    prior = inner[0:KPREV, 0:KPREV]
    coeffs = inner[0:KPREV, KPREV:]
    new = jnp.concatenate([inner[KPREV:, 0:KPREV], inner[KPREV:, KPREV:]], axis=0)
    mixed = dot(prior, coeffs, ((1,), (0,))) - 2.0 * coeffs
    gram = new + dot(coeffs, mixed, ((0,), (0,)))
    col_id = lax.broadcasted_iota(jnp.int32, (KPREV, 2 * KPREV), 1)
    unit = jnp.where(
        lax.broadcasted_iota(jnp.int32, (KPREV, KPREV), 0)
        == lax.broadcasted_iota(jnp.int32, (KPREV, KPREV), 1),
        1.0,
        0.0,
    )
    work = jnp.concatenate([gram, unit], axis=1)
    done = []
    for pivot in range(0, KPREV, PIVOTS):
        top = pivot // 8 * 8
        if pivot % 8 == 0 and pivot:
            done.append(work[:8])
            work = work[8:]
        at = pivot - top
        row_id = lax.broadcasted_iota(jnp.int32, work.shape, 0)
        columns = [
            jnp.broadcast_to(work[:, pivot + i : pivot + i + 1], work.shape) for i in range(PIVOTS)
        ]
        rows = [work[at + i : at + i + 1] for i in range(PIVOTS)]
        for i in range(PIVOTS):
            column = columns[i]
            factor = jnp.where(row_id > at + i, column * (1.0 / column[at + i : at + i + 1]), 0.0)
            work = work - factor * rows[i]
            for j in range(i + 1, PIVOTS):
                rows[j] = rows[j] - factor[at + j : at + j + 1] * rows[i]
                columns[j] = columns[j] - factor * columns[j][at + i : at + i + 1]
    work = jnp.concatenate(done + [work], axis=0)
    row_id = lax.broadcasted_iota(jnp.int32, (KPREV, 2 * KPREV), 0)
    diagonal = jnp.sum(jnp.where(row_id == col_id, work, 0.0), axis=1, keepdims=True)
    work = work / jnp.sqrt(diagonal)
    upper = work[:, :KPREV]
    triangle_out[...] = jnp.where(col_id[:, :KPREV] >= row_id[:, :KPREV], upper, 0.0)
    unknowns = 2 * 4 * 512 * 1024
    inverse = work[:, KPREV:] * math.sqrt(unknowns)
    weights = jnp.concatenate(
        [two_parts(-dot(inverse, coeffs, ((1,), (1,)))), two_parts(inverse)], axis=1
    )
    rows = result.reshape(2, KPREV * CELL_ROWS, LANES)
    stores = []
    for comp in range(COMPS):
        cells = slice(comp * COLS, (comp + 1) * COLS)
        for row in range(ROWS):
            vectors = jnp.concatenate([prior_parts[row, :, cells], new_parts[row, :, cells]], axis=0)
            both = jnp.dot(weights, vectors, preferred_element_type=jnp.float32)
            both = both[:KPREV] + both[KPREV:]
            where = pl.ds(comp * ROWS + row, KPREV, stride=CELL_ROWS)
            for half in range(2):
                rows[half, where, :] = both[:, half * LANES : (half + 1) * LANES]
        for half in range(2):
            copy = pltpu.make_async_copy(
                result.at[half, :, comp],
                basis_out.at[:, comp, :, pl.ds(half * LANES, LANES)],
                out_sems.at[comp, half],
            )
            copy.start()
            stores.append(copy)
    for copy in stores:
        copy.wait()


def two_parts(weights):
    high, low = split(weights)
    return jnp.concatenate(
        [
            jnp.concatenate([high, high], axis=1),
            jnp.concatenate([low, jnp.zeros_like(low)], axis=1),
        ],
        axis=0,
    )


def pairs_in(size, partner):
    return [(i, partner(i)) for i in range(size) if partner(i) is not None]


def row_exchange(value, bands, across):
    def partner(i):
        j = i + (1 if (i % 2 == 0) == (not across) else -1)
        return j if 0 <= j < bands else None

    return lax.ppermute(value, "band", pairs_in(bands, partner))


def col_exchange(value, cols, odd):
    def partner(i):
        j = i + (1 if (i % 2 == 0) == (not odd) else -1)
        return j if 0 <= j < cols else None

    return lax.ppermute(value, "col", pairs_in(cols, partner))


def sum_over_devices(value, bands, cols):
    def from_partner(mask):
        return lax.ppermute(
            value, ("band", "col"), [(i, i ^ mask) for i in range(bands * cols)]
        )

    rounds = [[cols]]
    at = 1
    while at < bands * cols:
        if at == cols:
            at *= 2
            continue
        if 4 * at <= bands * cols and 2 * at != cols:
            rounds.append([at, 2 * at, 3 * at])
            at *= 4
        else:
            last = (2 * at - 1) & ~(at // 4 - 1) if len(rounds) > 3 else at
            rounds.append([last])
            at *= 2
    for masks in rounds:
        value = value + sum(from_partner(mask) for mask in masks)
    return value


def per_device(prior_basis, coupling, velocity):
    bands, cols = lax.axis_size("band"), lax.axis_size("col")
    f32, bf16 = jnp.float32, jnp.bfloat16
    basis = prior_basis.reshape(KPREV * CELL_ROWS, COLS)
    slab, to_core, to_chip, edges = pl.pallas_call(
        pack_kernel,
        out_shape=(
            OUT((ROWS, SLAB, COLS), f32),
            OUT((WIDTH, SLAB, COLS), f32),
            OUT((WIDTH, SLAB, COLS), f32),
            OUT((PACKED, 8, LANES), f32),
        ),
        in_specs=[HBM, HBM, VMEM],
        out_specs=(VMEM, VMEM, VMEM, VMEM),
        scratch_shapes=[
            pltpu.VMEM((2, BLOCK * CELL_ROWS, LANES), f32),
            pltpu.VMEM((2, COUPLINGS * ROWS, LANES), f32),
            pltpu.SemaphoreType.DMA((4,)),
        ],
        compiler_params=pltpu.CompilerParams(vmem_limit_bytes=55 * 1024 * 1024),
        name="pack",
    )(basis, coupling.reshape(COUPLINGS * ROWS, COLS), velocity)
    from_chip = row_exchange(to_chip, bands, True)
    side_even = col_exchange(edges, cols, False)
    side_odd = col_exchange(edges, cols, True)
    from_core = row_exchange(to_core, bands, False)
    prior_parts, token = pl.pallas_call(
        prior_kernel,
        out_shape=(
            OUT((ROWS, BOTH, COMPS * COLS), bf16),
            OUT((8, LANES), f32),
        ),
        in_specs=[HBM],
        out_specs=(VMEM, VMEM),
        scratch_shapes=[
            pltpu.VMEM((2, KPREV * CELL_ROWS, LANES), f32),
            pltpu.SemaphoreType.DMA((KPREV // BLOCK, 2)),
        ],
        compiler_params=pltpu.CompilerParams(vmem_limit_bytes=8 * 1024 * 1024),
        cost_estimate=pl.CostEstimate(flops=4 * 10**9, bytes_accessed=8 * 10**6, transcendentals=0),
        name="prior",
    )(basis)
    sides = pl.pallas_call(
        merge_kernel,
        out_shape=OUT((PACKED, 8, LANES), f32),
        in_specs=[VMEM, VMEM, VMEM],
        out_specs=VMEM,
        compiler_params=pltpu.CompilerParams(vmem_limit_bytes=1024 * 1024),
        name="merge",
    )(side_even, side_odd, token)
    core_sides = row_exchange(sides, bands, False)
    chip_sides = row_exchange(sides, bands, True)
    new_parts, inner = pl.pallas_call(
        power_kernel,
        out_shape=(
            OUT((ROWS, BOTH, COMPS * COLS), bf16),
            jax.ShapeDtypeStruct((KPREV + KPREV // 2, BOTH), f32),
        ),
        in_specs=[ANY, ANY, ANY, VMEM, VMEM, VMEM, VMEM],
        out_specs=(VMEM, VMEM),
        scratch_shapes=[
            pltpu.VMEM((SPAN, PLANES, WIDE), f32),
            pltpu.VMEM((SPAN, PLANES, WIDE), f32),
            pltpu.VMEM((SPAN, COEFFS, WIDE), f32),
            pltpu.SemaphoreType.DMA((6,)),
        ],
        compiler_params=pltpu.CompilerParams(vmem_limit_bytes=24 * 1024 * 1024),
        name="powers",
    )(slab, from_core, from_chip, sides, core_sides, chip_sides, prior_parts)
    inner = sum_over_devices(inner, bands, cols)
    basis_next, triangle = pl.pallas_call(
        finish_kernel,
        out_shape=(
            jax.ShapeDtypeStruct((KPREV, COMPS, ROWS, COLS), f32),
            jax.ShapeDtypeStruct((KPREV, KPREV), f32),
        ),
        in_specs=[VMEM, VMEM, VMEM],
        out_specs=(ANY, VMEM),
        scratch_shapes=[
            pltpu.VMEM((2, KPREV, COMPS, ROWS, LANES), f32),
            pltpu.SemaphoreType.DMA((COMPS, 2)),
        ],
        compiler_params=pltpu.CompilerParams(vmem_limit_bytes=24 * 1024 * 1024),
        name="finish",
    )(inner, prior_parts, new_parts)
    return (basis_next.reshape(prior_basis.shape), triangle)


def solution(mesh):
    in_specs = (
        P(None, None, None, "band", "col"),
        P(None, None, None, "band", "col"),
        P(None, "band", "col"),
    )
    out_specs = (P(None, None, None, "band", "col"), P())
    return jax.shard_map(
        per_device, mesh=mesh, in_specs=in_specs, out_specs=out_specs, check_vma=False
    )
```

```python
import math

import jax
import jax.numpy as jnp
from jax import lax
from jax.experimental import pallas as pl
from jax.experimental.pallas import tpu as pltpu
from jax.sharding import PartitionSpec as P

BLOCK = 16
STEPS = 4
KPREV = 64
COMPS = 8
ROWS = 8
COLS = 256
LANES = 128
WIDTH = 4
PLANES = COMPS * BLOCK
COUPLINGS = 32
COEFFS = 40
SLAB = PLANES + COEFFS
TILES = SLAB // 8
PACKED = (TILES + 1) // 2
SPAN = ROWS + 2 * WIDTH
STENCIL = 48
MIXING = STENCIL + 8
BOTH = 2 * KPREV
PIVOTS = 8
CELL_ROWS = COMPS * ROWS
OUT = pltpu.VMEM

ANY = pl.BlockSpec(memory_space=pl.ANY)
VMEM = pl.BlockSpec(memory_space=pltpu.VMEM)
HBM = pl.BlockSpec(memory_space=pltpu.HBM)


def core_of_chip():
    return lax.rem(lax.axis_index("band"), 2)


def pack_kernel(basis, coupling, velocity, slab, core_out, chip_out, edges, start, mixing, sems):
    size = BLOCK * 2 * CELL_ROWS
    loads = [
        pltpu.make_async_copy(basis.at[pl.ds((KPREV // BLOCK - 1) * size, size), :], start, sems.at[0]),
        pltpu.make_async_copy(coupling, mixing, sems.at[1]),
    ]
    for copy in loads:
        copy.start()
    half_rows = 0.5 * velocity[0]
    half_cols = 0.5 * velocity[1]
    stencil = (0.15 - half_rows, 0.15 + half_rows, 0.15 - half_cols, 0.15 + half_cols)
    blank = jnp.zeros((4, COLS), jnp.float32)
    for row in range(ROWS):
        slab[row, PLANES + COUPLINGS :, :] = jnp.concatenate(
            [part[row : row + 1] for part in stencil] + [blank], axis=0
        )
    for copy in loads:
        copy.wait()
    for row in range(ROWS):
        for half in range(2):
            lanes = slice(half * LANES, (half + 1) * LANES)
            for comp in range(COMPS):
                slab[row, comp * BLOCK : (comp + 1) * BLOCK, lanes] = start[
                    pl.ds((2 * comp + half) * ROWS + row, BLOCK, stride=2 * CELL_ROWS), :
                ]
            slab[row, PLANES : PLANES + COUPLINGS, lanes] = mixing[
                pl.ds(half * ROWS + row, COUPLINGS, stride=2 * ROWS), :
            ]
    core = core_of_chip()
    for row in range(WIDTH):
        core_out[row] = slab[row + (1 - core) * WIDTH]
        chip_out[row] = slab[row + core * WIDTH]
    lane = lax.broadcasted_iota(jnp.int32, (8, LANES), 1)
    for packed in range(PACKED):
        total = jnp.zeros((8, LANES), jnp.float32)
        for half in range(2):
            tile = 2 * packed + half
            if tile >= TILES:
                continue
            for row in range(ROWS):
                group = half * ROWS + row
                first = slab[row, tile * 8 : tile * 8 + 8, 0:LANES]
                last = slab[row, tile * 8 : tile * 8 + 8, COLS - LANES : COLS]
                edge = pltpu.roll(jnp.where(lane < WIDTH, first, last), (8 * group + 4) % LANES, 1)
                total = jnp.where(lane // 8 == group, edge, total)
        edges[packed] = total


def split(value):
    high = value.astype(jnp.bfloat16)
    return high, (value - high.astype(jnp.float32)).astype(jnp.bfloat16)


def prior_kernel(basis, parts, token):
    def one_row(row, carry):
        for at in range(0, KPREV, BLOCK):
            for cells in range(2 * COMPS):
                start = (at * 2 * COMPS + cells) * ROWS
                high, low = split(basis[pl.ds(start + row, BLOCK, stride=2 * CELL_ROWS), :])
                lanes = pl.ds(cells * LANES, LANES)
                parts[row, pl.ds(at, BLOCK), lanes] = high
                parts[row, pl.ds(KPREV + at, BLOCK), lanes] = low
        return carry

    lax.fori_loop(0, ROWS, one_row, 0)
    token[...] = jnp.zeros_like(token)


def merge_kernel(side_even, side_odd, edges, after, sides):
    del after
    col_is_even = lax.rem(lax.axis_index("col"), 2) == 0
    is_low = lax.broadcasted_iota(jnp.int32, edges.shape, 2) % 8 < WIDTH
    by_right = jnp.where(col_is_even, side_even[...], side_odd[...])
    by_left = jnp.where(col_is_even, side_odd[...], side_even[...])
    sides[0:PACKED] = jnp.where(is_low, by_left, edges[...])
    sides[PACKED:] = jnp.where(is_low, edges[...], by_right)


def dot_rows(a, b):
    return lax.dot_general(a, b, (((1,), (1,)), ((), ())), preferred_element_type=jnp.float32)


def join_parts(total):
    crossed = total[KPREV:, 0:KPREV] + total[0:KPREV, KPREV:]
    return total[0:KPREV, 0:KPREV] + crossed + total[KPREV:, KPREV:]


def mixing_planes(coef):
    plane = lax.broadcasted_iota(jnp.int32, (16, coef.shape[1]), 0)
    real = coef[0:16] - jnp.where(plane % 5 == 0, 0.6, 0.0)
    imag = coef[16:32]
    return jnp.concatenate([real, imag - real, imag + real, coef[COUPLINGS:]], axis=0)


def advance(center, around, coeff, store):
    both = [center[field] + center[4 + field] for field in range(4)]
    for field in range(4):
        shared = around_real = around_imag = None
        for source in range(4):
            plane = field * 4 + source
            terms = (
                coeff(plane) * both[source],
                coeff(16 + plane) * center[source],
                coeff(32 + plane) * center[4 + source],
            )
            if source == 0:
                shared, around_imag, around_real = terms
            else:
                shared = shared + terms[0]
                around_imag = around_imag + terms[1]
                around_real = around_real + terms[2]
        store(field, around(field) + (shared - around_real))
        store(4 + field, around(4 + field) + (shared + around_imag))


def spread(value):
    return jnp.concatenate([value, value], axis=0)


def operator_row(cur, nxt, outside, mix, row):
    lane = lax.broadcasted_iota(jnp.int32, (BLOCK, LANES), 1)
    is_first, is_last = lane == 0, lane == LANES - 1

    def planes(comp):
        return pl.ds(comp * BLOCK, BLOCK)

    beyond = [pltpu.roll(outside[planes(comp), :], LANES - 4 - 8 * row, 1) for comp in range(COMPS)]
    for tile in range(2):
        lanes, others = pl.ds(tile * LANES, LANES), pl.ds((1 - tile) * LANES, LANES)
        center = [cur[row, planes(comp), lanes] for comp in range(COMPS)]

        def coeff(plane, tile=tile):
            return spread(mix[tile, row, pl.ds(plane, 8, stride=0), :])

        def around(comp, tile=tile, lanes=lanes, others=others, center=center, coeff=coeff):
            other = cur[row, planes(comp), others]
            after, before = (other, beyond[comp]) if tile == 0 else (beyond[comp], other)
            right = pltpu.roll(jnp.where(is_first, after, center[comp]), LANES - 1, 1)
            left = pltpu.roll(jnp.where(is_last, before, center[comp]), 1, 1)
            return (
                coeff(STENCIL) * cur[row + 1, planes(comp), lanes]
                + coeff(STENCIL + 1) * cur[row - 1, planes(comp), lanes]
                + coeff(STENCIL + 2) * right
                + coeff(STENCIL + 3) * left
            )

        def store(comp, value, lanes=lanes):
            nxt[row, planes(comp), lanes] = value

        advance(center, around, coeff, store)


def operator_strip(strip, strip_next, strip_mix, side):
    def planes(comp):
        return pl.ds(comp * BLOCK, BLOCK)

    def coeff(plane):
        return spread(strip_mix[side, pl.ds(plane, 8, stride=0), :])

    center = [strip[side, planes(comp), :] for comp in range(COMPS)]

    def around(comp):
        here = center[comp]
        return (
            coeff(STENCIL) * pltpu.roll(here, LANES - 8, 1)
            + coeff(STENCIL + 1) * pltpu.roll(here, 8, 1)
            + coeff(STENCIL + 2) * pltpu.roll(here, LANES - 1, 1)
            + coeff(STENCIL + 3) * pltpu.roll(here, 1, 1)
        )

    def store(comp, value):
        strip_next[side, planes(comp), :] = value

    advance(center, around, coeff, store)


def join_strips(strip, outside):
    lane = lax.broadcasted_iota(jnp.int32, outside.shape, 1)
    outside[...] = jnp.where(lane % 8 < WIDTH, strip[0], strip[1])


def power_kernel(
    slab, from_core, from_chip, sides, core_sides, chip_sides, prior_parts,
    parts, inner_out,
    ping, pong, coef, mix, strip_ping, strip_pong, strip_mix, outside, halo_sems,
):
    core = core_of_chip()
    is_first = core == 0
    core_at = pl.multiple_of((1 - core) * (SPAN - WIDTH), WIDTH)
    chip_at = pl.multiple_of(core * (SPAN - WIDTH), WIDTH)
    halos = []
    for index, (source, where, count) in enumerate(
        ((slab, WIDTH, ROWS), (from_core, core_at, WIDTH), (from_chip, chip_at, WIDTH))
    ):
        halos.append(
            pltpu.make_async_copy(
                source.at[:, pl.ds(0, PLANES), :],
                ping.at[pl.ds(where, count)],
                halo_sems.at[2 * index],
            )
        )
        halos.append(
            pltpu.make_async_copy(
                source.at[:, pl.ds(PLANES, COEFFS), :],
                coef.at[pl.ds(where, count)],
                halo_sems.at[2 * index + 1],
            )
        )
    for copy in halos:
        copy.start()
    lane = lax.broadcasted_iota(jnp.int32, (8, LANES), 1)
    for side in range(2):
        strip_coef = []
        for tile in range(TILES):
            packed, at = side * PACKED + tile // 2, tile % 2 * (LANES // 2)
            by_core, by_chip = core_sides[packed], chip_sides[packed]
            above = pltpu.roll(jnp.where(is_first, by_core, by_chip), (3 * LANES // 4 - at) % LANES, 1)
            below = pltpu.roll(
                jnp.where(is_first, by_chip, by_core), (LANES - at - LANES // 4) % LANES, 1
            )
            own = pltpu.roll(sides[packed], (LANES + LANES // 4 - at) % LANES, 1)
            strip = jnp.where(lane < LANES // 4, below, jnp.where(lane < 3 * LANES // 4, own, above))
            if tile < PLANES // 8:
                strip_ping[side, tile * 8 : tile * 8 + 8] = strip
            else:
                strip_coef.append(strip)
        strip_mix[side, 0:MIXING] = mixing_planes(jnp.concatenate(strip_coef, axis=0))
    for copy in halos:
        copy.wait()

    def one_mix(row, carry):
        for tile in range(2):
            mix[tile, row, 0:MIXING] = mixing_planes(coef[row, :, pl.ds(tile * LANES, LANES)])
        return carry

    lax.fori_loop(0, SPAN, one_mix, 0, unroll=4)
    buffers = ((ping, strip_ping), (pong, strip_pong))
    for step in range(1, STEPS + 1):
        (cur, strip), (nxt, strip_next) = buffers[(step - 1) % 2], buffers[step % 2]

        join_strips(strip, outside)

        def one_row(row, carry, cur=cur, nxt=nxt):
            operator_row(cur, nxt, outside, mix, row)
            return carry

        lax.fori_loop(step, SPAN - step, one_row, 0, unroll=True)
        if step < STEPS:
            for side in range(2):
                operator_strip(strip, strip_next, strip_mix, side)

        def one_split(row, carry, nxt=nxt, step=step):
            at = (step - 1) * BLOCK
            for comp in range(COMPS):
                high, low = split(nxt[row + WIDTH, pl.ds(comp * BLOCK, BLOCK), :])
                parts[row, pl.ds(at, BLOCK), pl.ds(comp * COLS, COLS)] = high
                parts[row, pl.ds(KPREV + at, BLOCK), pl.ds(comp * COLS, COLS)] = low
            return carry

        lax.fori_loop(0, ROWS, one_split, 0, unroll=True)
    total = 0.0
    for row in range(ROWS):
        block = jnp.concatenate([prior_parts[row], parts[row]], axis=0)
        total = total + dot_rows(block, block)
    inner_out[0:KPREV] = jnp.concatenate(
        [join_parts(total[:BOTH, :BOTH]), join_parts(total[:BOTH, BOTH:])], axis=1
    )
    new = join_parts(total[BOTH:, BOTH:])
    inner_out[KPREV:] = jnp.concatenate([new[: KPREV // 2], new[KPREV // 2 :]], axis=1)


def finish_kernel(inner, prior_parts, new_parts, basis_out, triangle_out, result, out_sems):
    def dot(a, b, dims):
        return lax.dot_general(
            a, b, (dims, ((), ())), precision=lax.Precision.HIGHEST, preferred_element_type=jnp.float32
        )

    prior = inner[0:KPREV, 0:KPREV]
    coeffs = inner[0:KPREV, KPREV:]
    new = jnp.concatenate([inner[KPREV:, 0:KPREV], inner[KPREV:, KPREV:]], axis=0)
    mixed = dot(prior, coeffs, ((1,), (0,))) - 2.0 * coeffs
    gram = new + dot(coeffs, mixed, ((0,), (0,)))
    col_id = lax.broadcasted_iota(jnp.int32, (KPREV, 2 * KPREV), 1)
    unit = jnp.where(
        lax.broadcasted_iota(jnp.int32, (KPREV, KPREV), 0)
        == lax.broadcasted_iota(jnp.int32, (KPREV, KPREV), 1),
        1.0,
        0.0,
    )
    work = jnp.concatenate([gram, unit], axis=1)
    done = []
    for pivot in range(0, KPREV, PIVOTS):
        top = pivot // 8 * 8
        if pivot % 8 == 0 and pivot:
            done.append(work[:8])
            work = work[8:]
        at = pivot - top
        row_id = lax.broadcasted_iota(jnp.int32, work.shape, 0)
        columns = [
            jnp.broadcast_to(work[:, pivot + i : pivot + i + 1], work.shape) for i in range(PIVOTS)
        ]
        rows = [work[at + i : at + i + 1] for i in range(PIVOTS)]
        for i in range(PIVOTS):
            column = columns[i]
            factor = jnp.where(row_id > at + i, column * (1.0 / column[at + i : at + i + 1]), 0.0)
            work = work - factor * rows[i]
            for j in range(i + 1, PIVOTS):
                rows[j] = rows[j] - factor[at + j : at + j + 1] * rows[i]
                columns[j] = columns[j] - factor * columns[j][at + i : at + i + 1]
    work = jnp.concatenate(done + [work], axis=0)
    row_id = lax.broadcasted_iota(jnp.int32, (KPREV, 2 * KPREV), 0)
    diagonal = jnp.sum(jnp.where(row_id == col_id, work, 0.0), axis=1, keepdims=True)
    work = work / jnp.sqrt(diagonal)
    upper = work[:, :KPREV]
    triangle_out[...] = jnp.where(col_id[:, :KPREV] >= row_id[:, :KPREV], upper, 0.0)
    unknowns = 2 * 4 * 512 * 1024
    inverse = work[:, KPREV:] * math.sqrt(unknowns)
    weights = jnp.concatenate(
        [two_parts(-dot(inverse, coeffs, ((1,), (1,)))), two_parts(inverse)], axis=1
    )
    rows = result.reshape(KPREV * 2 * CELL_ROWS, LANES)
    stores = []
    for comp in range(COMPS):
        cells = slice(comp * COLS, (comp + 1) * COLS)
        for row in range(ROWS):
            vectors = jnp.concatenate([prior_parts[row, :, cells], new_parts[row, :, cells]], axis=0)
            both = jnp.dot(weights, vectors, preferred_element_type=jnp.float32)
            both = both[:KPREV] + both[KPREV:]
            for half in range(2):
                where = pl.ds((comp * 2 + half) * ROWS + row, KPREV, stride=2 * CELL_ROWS)
                rows[where, :] = both[:, half * LANES : (half + 1) * LANES]
        copy = pltpu.make_async_copy(result.at[:, comp], basis_out.at[:, comp], out_sems.at[comp])
        copy.start()
        stores.append(copy)
    for copy in stores:
        copy.wait()


def two_parts(weights):
    high, low = split(weights)
    return jnp.concatenate(
        [
            jnp.concatenate([high, high], axis=1),
            jnp.concatenate([low, jnp.zeros_like(low)], axis=1),
        ],
        axis=0,
    )


def pairs_in(size, partner):
    return [(i, partner(i)) for i in range(size) if partner(i) is not None]


def row_exchange(value, bands, across):
    def partner(i):
        j = i + (1 if (i % 2 == 0) == (not across) else -1)
        return j if 0 <= j < bands else None

    return lax.ppermute(value, "band", pairs_in(bands, partner))


def col_exchange(value, cols, odd):
    def partner(i):
        j = i + (1 if (i % 2 == 0) == (not odd) else -1)
        return j if 0 <= j < cols else None

    return lax.ppermute(value, "col", pairs_in(cols, partner))


def sum_over_devices(value, bands, cols):
    def from_partner(mask):
        return lax.ppermute(
            value, ("band", "col"), [(i, i ^ mask) for i in range(bands * cols)]
        )

    rounds = [[cols]]
    at = 1
    while at < bands * cols:
        if at == cols:
            at *= 2
            continue
        if 4 * at <= bands * cols and 2 * at != cols:
            rounds.append([at, 2 * at, 3 * at])
            at *= 4
        else:
            last = (2 * at - 1) & ~(at // 4 - 1) if len(rounds) > 3 else at
            rounds.append([last])
            at *= 2
    for masks in rounds:
        value = value + sum(from_partner(mask) for mask in masks)
    return value


def per_device(prior_basis, coupling, velocity):
    bands, cols = lax.axis_size("band"), lax.axis_size("col")
    f32, bf16 = jnp.float32, jnp.bfloat16
    basis = prior_basis.reshape(KPREV, COMPS, ROWS, 2, LANES).swapaxes(2, 3)
    slab, to_core, to_chip, edges = pl.pallas_call(
        pack_kernel,
        out_shape=(
            OUT((ROWS, SLAB, COLS), f32),
            OUT((WIDTH, SLAB, COLS), f32),
            OUT((WIDTH, SLAB, COLS), f32),
            OUT((PACKED, 8, LANES), f32),
        ),
        in_specs=[HBM, HBM, VMEM],
        out_specs=(VMEM, VMEM, VMEM, VMEM),
        scratch_shapes=[
            pltpu.VMEM((BLOCK * CELL_ROWS * 2, LANES), f32),
            pltpu.VMEM((COUPLINGS * ROWS * 2, LANES), f32),
            pltpu.SemaphoreType.DMA((2,)),
        ],
        compiler_params=pltpu.CompilerParams(vmem_limit_bytes=55 * 1024 * 1024),
        name="pack",
    )(
        basis.reshape(KPREV * CELL_ROWS * 2, LANES),
        coupling.reshape(COUPLINGS, ROWS, 2, LANES).swapaxes(1, 2).reshape(COUPLINGS * ROWS * 2, LANES),
        velocity,
    )
    from_chip = row_exchange(to_chip, bands, True)
    side_even = col_exchange(edges, cols, False)
    side_odd = col_exchange(edges, cols, True)
    from_core = row_exchange(to_core, bands, False)
    prior_parts, token = pl.pallas_call(
        prior_kernel,
        out_shape=(
            OUT((ROWS, BOTH, COMPS * COLS), bf16),
            OUT((8, LANES), f32),
        ),
        in_specs=[VMEM],
        out_specs=(VMEM, VMEM),
        compiler_params=pltpu.CompilerParams(vmem_limit_bytes=8 * 1024 * 1024),
        cost_estimate=pl.CostEstimate(flops=4 * 10**9, bytes_accessed=8 * 10**6, transcendentals=0),
        name="prior",
    )(basis.reshape(KPREV * CELL_ROWS * 2, LANES))
    sides = pl.pallas_call(
        merge_kernel,
        out_shape=OUT((2 * PACKED, 8, LANES), f32),
        in_specs=[VMEM, VMEM, VMEM, VMEM],
        out_specs=VMEM,
        compiler_params=pltpu.CompilerParams(vmem_limit_bytes=1024 * 1024),
        name="merge",
    )(side_even, side_odd, edges, token)
    core_sides = row_exchange(sides, bands, False)
    chip_sides = row_exchange(sides, bands, True)
    new_parts, inner = pl.pallas_call(
        power_kernel,
        out_shape=(
            OUT((ROWS, BOTH, COMPS * COLS), bf16),
            jax.ShapeDtypeStruct((KPREV + KPREV // 2, BOTH), f32),
        ),
        in_specs=[ANY, ANY, ANY, VMEM, VMEM, VMEM, VMEM],
        out_specs=(VMEM, VMEM),
        scratch_shapes=[
            pltpu.VMEM((SPAN, PLANES, COLS), f32),
            pltpu.VMEM((SPAN, PLANES, COLS), f32),
            pltpu.VMEM((SPAN, COEFFS, COLS), f32),
            pltpu.VMEM((2, SPAN, MIXING + 8, LANES), f32),
            pltpu.VMEM((2, PLANES, LANES), f32),
            pltpu.VMEM((2, PLANES, LANES), f32),
            pltpu.VMEM((2, MIXING + 8, LANES), f32),
            pltpu.VMEM((PLANES, LANES), f32),
            pltpu.SemaphoreType.DMA((6,)),
        ],
        compiler_params=pltpu.CompilerParams(vmem_limit_bytes=24 * 1024 * 1024),
        name="powers",
    )(slab, from_core, from_chip, sides, core_sides, chip_sides, prior_parts)
    inner = sum_over_devices(inner, bands, cols)
    basis_next, triangle = pl.pallas_call(
        finish_kernel,
        out_shape=(
            jax.ShapeDtypeStruct((KPREV, COMPS, 2, ROWS, LANES), f32),
            jax.ShapeDtypeStruct((KPREV, KPREV), f32),
        ),
        in_specs=[VMEM, VMEM, VMEM],
        out_specs=(ANY, VMEM),
        scratch_shapes=[
            pltpu.VMEM((KPREV, COMPS, 2, ROWS, LANES), f32),
            pltpu.SemaphoreType.DMA((COMPS,)),
        ],
        compiler_params=pltpu.CompilerParams(vmem_limit_bytes=24 * 1024 * 1024),
        name="finish",
    )(inner, prior_parts, new_parts)
    basis_next = basis_next.swapaxes(2, 3).reshape(prior_basis.shape)
    return (basis_next, triangle)


def solution(mesh):
    in_specs = (
        P(None, None, None, "band", "col"),
        P(None, None, None, "band", "col"),
        P(None, "band", "col"),
    )
    out_specs = (P(None, None, None, "band", "col"), P())
    return jax.shard_map(
        per_device, mesh=mesh, in_specs=in_specs, out_specs=out_specs, check_vma=False
    )
```

```python
import math

import jax
import jax.numpy as jnp
from jax import lax
from jax.experimental import pallas as pl
from jax.experimental.pallas import tpu as pltpu
from jax.sharding import PartitionSpec as P

BLOCK = 16
STEPS = 4
KPREV = 64
COMPS = 8
ROWS = 8
COLS = 256
LANES = 128
WIDTH = 4
PLANES = COMPS * BLOCK
COUPLINGS = 32
COEFFS = 40
SLAB = PLANES + COEFFS
TILES = SLAB // 8
PACKED = (TILES + 1) // 2
SPAN = ROWS + 2 * WIDTH
STENCIL = 48
MIXING = STENCIL + 8
BOTH = 2 * KPREV
PIVOTS = 8
CELL_ROWS = COMPS * ROWS
OUT = pltpu.VMEM

ANY = pl.BlockSpec(memory_space=pl.ANY)
VMEM = pl.BlockSpec(memory_space=pltpu.VMEM)
HBM = pl.BlockSpec(memory_space=pltpu.HBM)


def core_of_chip():
    return lax.rem(lax.axis_index("band"), 2)


def pack_kernel(basis, coupling, velocity, slab, core_out, chip_out, edges, start, mixing, sems):
    size = BLOCK * 2 * CELL_ROWS
    loads = [
        pltpu.make_async_copy(basis.at[pl.ds((KPREV // BLOCK - 1) * size, size), :], start, sems.at[0]),
        pltpu.make_async_copy(coupling, mixing, sems.at[1]),
    ]
    for copy in loads:
        copy.start()
    half_rows = 0.5 * velocity[0]
    half_cols = 0.5 * velocity[1]
    stencil = (0.15 - half_rows, 0.15 + half_rows, 0.15 - half_cols, 0.15 + half_cols)
    blank = jnp.zeros((4, COLS), jnp.float32)
    for row in range(ROWS):
        slab[row, PLANES + COUPLINGS :, :] = jnp.concatenate(
            [part[row : row + 1] for part in stencil] + [blank], axis=0
        )
    for copy in loads:
        copy.wait()
    for row in range(ROWS):
        for half in range(2):
            lanes = slice(half * LANES, (half + 1) * LANES)
            for comp in range(COMPS):
                slab[row, comp * BLOCK : (comp + 1) * BLOCK, lanes] = start[
                    pl.ds((2 * comp + half) * ROWS + row, BLOCK, stride=2 * CELL_ROWS), :
                ]
            slab[row, PLANES : PLANES + COUPLINGS, lanes] = mixing[
                pl.ds(half * ROWS + row, COUPLINGS, stride=2 * ROWS), :
            ]
    core = core_of_chip()
    for row in range(WIDTH):
        core_out[row] = slab[row + (1 - core) * WIDTH]
        chip_out[row] = slab[row + core * WIDTH]
    lane = lax.broadcasted_iota(jnp.int32, (8, LANES), 1)
    for packed in range(PACKED):
        total = jnp.zeros((8, LANES), jnp.float32)
        for half in range(2):
            tile = 2 * packed + half
            if tile >= TILES:
                continue
            for row in range(ROWS):
                group = half * ROWS + row
                first = slab[row, tile * 8 : tile * 8 + 8, 0:LANES]
                last = slab[row, tile * 8 : tile * 8 + 8, COLS - LANES : COLS]
                edge = pltpu.roll(jnp.where(lane < WIDTH, first, last), (8 * group + 4) % LANES, 1)
                total = jnp.where(lane // 8 == group, edge, total)
        edges[packed] = total


def split(value):
    high = value.astype(jnp.bfloat16)
    return high, (value - high.astype(jnp.float32)).astype(jnp.bfloat16)


def prior_kernel(basis, parts, token):
    def one_row(row, carry):
        for at in range(0, KPREV, BLOCK):
            for cells in range(2 * COMPS):
                start = (at * 2 * COMPS + cells) * ROWS
                high, low = split(basis[pl.ds(start + row, BLOCK, stride=2 * CELL_ROWS), :])
                lanes = pl.ds(cells * LANES, LANES)
                parts[row, pl.ds(at, BLOCK), lanes] = high
                parts[row, pl.ds(KPREV + at, BLOCK), lanes] = low
        return carry

    lax.fori_loop(0, ROWS, one_row, 0, unroll=4)
    token[...] = jnp.zeros_like(token)


def merge_kernel(side_even, side_odd, edges, after, sides):
    del after
    col_is_even = lax.rem(lax.axis_index("col"), 2) == 0
    is_low = lax.broadcasted_iota(jnp.int32, edges.shape, 2) % 8 < WIDTH
    by_right = jnp.where(col_is_even, side_even[...], side_odd[...])
    by_left = jnp.where(col_is_even, side_odd[...], side_even[...])
    sides[0:PACKED] = jnp.where(is_low, by_left, edges[...])
    sides[PACKED:] = jnp.where(is_low, edges[...], by_right)


def dot_rows(a, b):
    return lax.dot_general(a, b, (((1,), (1,)), ((), ())), preferred_element_type=jnp.float32)


def join_parts(total):
    crossed = total[KPREV:, 0:KPREV] + total[0:KPREV, KPREV:]
    return total[0:KPREV, 0:KPREV] + crossed + total[KPREV:, KPREV:]


def mixing_planes(coef):
    plane = lax.broadcasted_iota(jnp.int32, (16, coef.shape[1]), 0)
    real = coef[0:16] - jnp.where(plane % 5 == 0, 0.6, 0.0)
    imag = coef[16:32]
    return jnp.concatenate([real, imag - real, imag + real, coef[COUPLINGS:]], axis=0)


def advance(center, around, coeff, store):
    both = [center[field] + center[4 + field] for field in range(4)]
    for field in range(4):
        shared = around_real = around_imag = None
        for source in range(4):
            plane = field * 4 + source
            terms = (
                coeff(plane) * both[source],
                coeff(16 + plane) * center[source],
                coeff(32 + plane) * center[4 + source],
            )
            if source == 0:
                shared, around_imag, around_real = terms
            else:
                shared = shared + terms[0]
                around_imag = around_imag + terms[1]
                around_real = around_real + terms[2]
        store(field, around(field) + (shared - around_real))
        store(4 + field, around(4 + field) + (shared + around_imag))


def spread(value):
    return jnp.concatenate([value, value], axis=0)


def operator_row(cur, nxt, outside, mix, row):
    lane = lax.broadcasted_iota(jnp.int32, (BLOCK, LANES), 1)
    is_first, is_last = lane == 0, lane == LANES - 1

    def planes(comp):
        return pl.ds(comp * BLOCK, BLOCK)

    beyond = [pltpu.roll(outside[planes(comp), :], LANES - 4 - 8 * row, 1) for comp in range(COMPS)]
    for tile in range(2):
        lanes, others = pl.ds(tile * LANES, LANES), pl.ds((1 - tile) * LANES, LANES)
        center = [cur[row, planes(comp), lanes] for comp in range(COMPS)]

        def coeff(plane, tile=tile):
            return spread(mix[tile, row, pl.ds(plane, 8, stride=0), :])

        def around(comp, tile=tile, lanes=lanes, others=others, center=center, coeff=coeff):
            other = cur[row, planes(comp), others]
            after, before = (other, beyond[comp]) if tile == 0 else (beyond[comp], other)
            right = pltpu.roll(jnp.where(is_first, after, center[comp]), LANES - 1, 1)
            left = pltpu.roll(jnp.where(is_last, before, center[comp]), 1, 1)
            return (
                coeff(STENCIL) * cur[row + 1, planes(comp), lanes]
                + coeff(STENCIL + 1) * cur[row - 1, planes(comp), lanes]
                + coeff(STENCIL + 2) * right
                + coeff(STENCIL + 3) * left
            )

        def store(comp, value, lanes=lanes):
            nxt[row, planes(comp), lanes] = value

        advance(center, around, coeff, store)


def operator_strip(strip, strip_next, strip_mix, side):
    def planes(comp):
        return pl.ds(comp * BLOCK, BLOCK)

    def coeff(plane):
        return spread(strip_mix[side, pl.ds(plane, 8, stride=0), :])

    center = [strip[side, planes(comp), :] for comp in range(COMPS)]

    def around(comp):
        here = center[comp]
        return (
            coeff(STENCIL) * pltpu.roll(here, LANES - 8, 1)
            + coeff(STENCIL + 1) * pltpu.roll(here, 8, 1)
            + coeff(STENCIL + 2) * pltpu.roll(here, LANES - 1, 1)
            + coeff(STENCIL + 3) * pltpu.roll(here, 1, 1)
        )

    def store(comp, value):
        strip_next[side, planes(comp), :] = value

    advance(center, around, coeff, store)


def join_strips(strip, outside):
    lane = lax.broadcasted_iota(jnp.int32, outside.shape, 1)
    outside[...] = jnp.where(lane % 8 < WIDTH, strip[0], strip[1])


def power_kernel(
    slab, from_core, from_chip, sides, core_sides, chip_sides, prior_parts,
    parts, inner_out,
    ping, pong, coef, mix, strip_ping, strip_pong, strip_mix, outside, halo_sems,
):
    core = core_of_chip()
    is_first = core == 0
    core_at = pl.multiple_of((1 - core) * (SPAN - WIDTH), WIDTH)
    chip_at = pl.multiple_of(core * (SPAN - WIDTH), WIDTH)
    halos = []
    for index, (source, where, count) in enumerate(
        ((slab, WIDTH, ROWS), (from_core, core_at, WIDTH), (from_chip, chip_at, WIDTH))
    ):
        halos.append(
            pltpu.make_async_copy(
                source.at[:, pl.ds(0, PLANES), :],
                ping.at[pl.ds(where, count)],
                halo_sems.at[2 * index],
            )
        )
        halos.append(
            pltpu.make_async_copy(
                source.at[:, pl.ds(PLANES, COEFFS), :],
                coef.at[pl.ds(where, count)],
                halo_sems.at[2 * index + 1],
            )
        )
    for copy in halos:
        copy.start()
    lane = lax.broadcasted_iota(jnp.int32, (8, LANES), 1)
    for side in range(2):
        strip_coef = []
        for tile in range(TILES):
            packed, at = side * PACKED + tile // 2, tile % 2 * (LANES // 2)
            by_core, by_chip = core_sides[packed], chip_sides[packed]
            above = pltpu.roll(jnp.where(is_first, by_core, by_chip), (3 * LANES // 4 - at) % LANES, 1)
            below = pltpu.roll(
                jnp.where(is_first, by_chip, by_core), (LANES - at - LANES // 4) % LANES, 1
            )
            own = pltpu.roll(sides[packed], (LANES + LANES // 4 - at) % LANES, 1)
            strip = jnp.where(lane < LANES // 4, below, jnp.where(lane < 3 * LANES // 4, own, above))
            if tile < PLANES // 8:
                strip_ping[side, tile * 8 : tile * 8 + 8] = strip
            else:
                strip_coef.append(strip)
        strip_mix[side, 0:MIXING] = mixing_planes(jnp.concatenate(strip_coef, axis=0))
    for copy in halos:
        copy.wait()

    def one_mix(row, carry):
        for tile in range(2):
            mix[tile, row, 0:MIXING] = mixing_planes(coef[row, :, pl.ds(tile * LANES, LANES)])
        return carry

    lax.fori_loop(0, SPAN, one_mix, 0, unroll=4)
    buffers = ((ping, strip_ping), (pong, strip_pong))
    for step in range(1, STEPS + 1):
        (cur, strip), (nxt, strip_next) = buffers[(step - 1) % 2], buffers[step % 2]

        join_strips(strip, outside)

        def one_row(row, carry, cur=cur, nxt=nxt):
            operator_row(cur, nxt, outside, mix, row)
            return carry

        lax.fori_loop(step, SPAN - step, one_row, 0, unroll=True)
        if step < STEPS:
            for side in range(2):
                operator_strip(strip, strip_next, strip_mix, side)

        def one_split(row, carry, nxt=nxt, step=step):
            at = (step - 1) * BLOCK
            for comp in range(COMPS):
                high, low = split(nxt[row + WIDTH, pl.ds(comp * BLOCK, BLOCK), :])
                parts[row, pl.ds(at, BLOCK), pl.ds(comp * COLS, COLS)] = high
                parts[row, pl.ds(KPREV + at, BLOCK), pl.ds(comp * COLS, COLS)] = low
            return carry

        lax.fori_loop(0, ROWS, one_split, 0, unroll=True)
    total = 0.0
    for row in range(ROWS):
        block = jnp.concatenate([prior_parts[row], parts[row]], axis=0)
        total = total + dot_rows(block, block)
    inner_out[0:KPREV] = jnp.concatenate(
        [join_parts(total[:BOTH, :BOTH]), join_parts(total[:BOTH, BOTH:])], axis=1
    )
    new = join_parts(total[BOTH:, BOTH:])
    inner_out[KPREV:] = jnp.concatenate([new[: KPREV // 2], new[KPREV // 2 :]], axis=1)


def finish_kernel(inner, prior_parts, new_parts, basis_out, triangle_out, result, out_sems):
    def dot(a, b, dims):
        return lax.dot_general(
            a, b, (dims, ((), ())), precision=lax.Precision.HIGHEST, preferred_element_type=jnp.float32
        )

    prior = inner[0:KPREV, 0:KPREV]
    coeffs = inner[0:KPREV, KPREV:]
    new = jnp.concatenate([inner[KPREV:, 0:KPREV], inner[KPREV:, KPREV:]], axis=0)
    mixed = dot(prior, coeffs, ((1,), (0,))) - 2.0 * coeffs
    gram = new + dot(coeffs, mixed, ((0,), (0,)))
    col_id = lax.broadcasted_iota(jnp.int32, (KPREV, 2 * KPREV), 1)
    unit = jnp.where(
        lax.broadcasted_iota(jnp.int32, (KPREV, KPREV), 0)
        == lax.broadcasted_iota(jnp.int32, (KPREV, KPREV), 1),
        1.0,
        0.0,
    )
    work = jnp.concatenate([gram, unit], axis=1)
    done = []
    for pivot in range(0, KPREV, PIVOTS):
        top = pivot // 8 * 8
        if pivot % 8 == 0 and pivot:
            done.append(work[:8])
            work = work[8:]
        at = pivot - top
        row_id = lax.broadcasted_iota(jnp.int32, work.shape, 0)
        columns = [
            jnp.broadcast_to(work[:, pivot + i : pivot + i + 1], work.shape) for i in range(PIVOTS)
        ]
        rows = [work[at + i : at + i + 1] for i in range(PIVOTS)]
        for i in range(PIVOTS):
            column = columns[i]
            factor = jnp.where(row_id > at + i, column * (1.0 / column[at + i : at + i + 1]), 0.0)
            work = work - factor * rows[i]
            for j in range(i + 1, PIVOTS):
                rows[j] = rows[j] - factor[at + j : at + j + 1] * rows[i]
                columns[j] = columns[j] - factor * columns[j][at + i : at + i + 1]
    work = jnp.concatenate(done + [work], axis=0)
    row_id = lax.broadcasted_iota(jnp.int32, (KPREV, 2 * KPREV), 0)
    diagonal = jnp.sum(jnp.where(row_id == col_id, work, 0.0), axis=1, keepdims=True)
    work = work / jnp.sqrt(diagonal)
    upper = work[:, :KPREV]
    triangle_out[...] = jnp.where(col_id[:, :KPREV] >= row_id[:, :KPREV], upper, 0.0)
    unknowns = 2 * 4 * 512 * 1024
    inverse = work[:, KPREV:] * math.sqrt(unknowns)
    weights = jnp.concatenate(
        [two_parts(-dot(inverse, coeffs, ((1,), (1,)))), two_parts(inverse)], axis=1
    )
    rows = result.reshape(KPREV * 2 * CELL_ROWS, LANES)
    stores = []
    for comp in range(COMPS):
        cells = slice(comp * COLS, (comp + 1) * COLS)
        for row in range(ROWS):
            vectors = jnp.concatenate([prior_parts[row, :, cells], new_parts[row, :, cells]], axis=0)
            both = jnp.dot(weights, vectors, preferred_element_type=jnp.float32)
            both = both[:KPREV] + both[KPREV:]
            for half in range(2):
                where = pl.ds((comp * 2 + half) * ROWS + row, KPREV, stride=2 * CELL_ROWS)
                rows[where, :] = both[:, half * LANES : (half + 1) * LANES]
        copy = pltpu.make_async_copy(result.at[:, comp], basis_out.at[:, comp], out_sems.at[comp])
        copy.start()
        stores.append(copy)
    for copy in stores:
        copy.wait()


def two_parts(weights):
    high, low = split(weights)
    return jnp.concatenate(
        [
            jnp.concatenate([high, high], axis=1),
            jnp.concatenate([low, jnp.zeros_like(low)], axis=1),
        ],
        axis=0,
    )


def pairs_in(size, partner):
    return [(i, partner(i)) for i in range(size) if partner(i) is not None]


def row_exchange(value, bands, across):
    def partner(i):
        j = i + (1 if (i % 2 == 0) == (not across) else -1)
        return j if 0 <= j < bands else None

    return lax.ppermute(value, "band", pairs_in(bands, partner))


def col_exchange(value, cols, odd):
    def partner(i):
        j = i + (1 if (i % 2 == 0) == (not odd) else -1)
        return j if 0 <= j < cols else None

    return lax.ppermute(value, "col", pairs_in(cols, partner))


def sum_over_devices(value, bands, cols):
    def from_partner(mask):
        return lax.ppermute(
            value, ("band", "col"), [(i, i ^ mask) for i in range(bands * cols)]
        )

    rounds = [[cols]]
    at = 1
    while at < bands * cols:
        if at == cols:
            at *= 2
            continue
        if 4 * at <= bands * cols and 2 * at != cols:
            rounds.append([at, 2 * at, 3 * at])
            at *= 4
        else:
            last = (2 * at - 1) & ~(at // 4 - 1) if len(rounds) > 3 else at
            rounds.append([last])
            at *= 2
    for masks in rounds:
        value = value + sum(from_partner(mask) for mask in masks)
    return value


def per_device(prior_basis, coupling, velocity):
    bands, cols = lax.axis_size("band"), lax.axis_size("col")
    f32, bf16 = jnp.float32, jnp.bfloat16
    basis = prior_basis.reshape(KPREV, COMPS, ROWS, 2, LANES).swapaxes(2, 3)
    slab, to_core, to_chip, edges = pl.pallas_call(
        pack_kernel,
        out_shape=(
            OUT((ROWS, SLAB, COLS), f32),
            OUT((WIDTH, SLAB, COLS), f32),
            OUT((WIDTH, SLAB, COLS), f32),
            OUT((PACKED, 8, LANES), f32),
        ),
        in_specs=[HBM, HBM, VMEM],
        out_specs=(VMEM, VMEM, VMEM, VMEM),
        scratch_shapes=[
            pltpu.VMEM((BLOCK * CELL_ROWS * 2, LANES), f32),
            pltpu.VMEM((COUPLINGS * ROWS * 2, LANES), f32),
            pltpu.SemaphoreType.DMA((2,)),
        ],
        compiler_params=pltpu.CompilerParams(vmem_limit_bytes=55 * 1024 * 1024),
        name="pack",
    )(
        basis.reshape(KPREV * CELL_ROWS * 2, LANES),
        coupling.reshape(COUPLINGS, ROWS, 2, LANES).swapaxes(1, 2).reshape(COUPLINGS * ROWS * 2, LANES),
        velocity,
    )
    from_chip = row_exchange(to_chip, bands, True)
    side_even = col_exchange(edges, cols, False)
    side_odd = col_exchange(edges, cols, True)
    from_core = row_exchange(to_core, bands, False)
    prior_parts, token = pl.pallas_call(
        prior_kernel,
        out_shape=(
            OUT((ROWS, BOTH, COMPS * COLS), bf16),
            OUT((8, LANES), f32),
        ),
        in_specs=[VMEM],
        out_specs=(VMEM, VMEM),
        compiler_params=pltpu.CompilerParams(vmem_limit_bytes=8 * 1024 * 1024),
        cost_estimate=pl.CostEstimate(flops=4 * 10**9, bytes_accessed=8 * 10**6, transcendentals=0),
        name="prior",
    )(basis.reshape(KPREV * CELL_ROWS * 2, LANES))
    sides = pl.pallas_call(
        merge_kernel,
        out_shape=OUT((2 * PACKED, 8, LANES), f32),
        in_specs=[VMEM, VMEM, VMEM, VMEM],
        out_specs=VMEM,
        compiler_params=pltpu.CompilerParams(vmem_limit_bytes=1024 * 1024),
        name="merge",
    )(side_even, side_odd, edges, token)
    core_sides = row_exchange(sides, bands, False)
    chip_sides = row_exchange(sides, bands, True)
    new_parts, inner = pl.pallas_call(
        power_kernel,
        out_shape=(
            OUT((ROWS, BOTH, COMPS * COLS), bf16),
            jax.ShapeDtypeStruct((KPREV + KPREV // 2, BOTH), f32),
        ),
        in_specs=[ANY, ANY, ANY, VMEM, VMEM, VMEM, VMEM],
        out_specs=(VMEM, VMEM),
        scratch_shapes=[
            pltpu.VMEM((SPAN, PLANES, COLS), f32),
            pltpu.VMEM((SPAN, PLANES, COLS), f32),
            pltpu.VMEM((SPAN, COEFFS, COLS), f32),
            pltpu.VMEM((2, SPAN, MIXING + 8, LANES), f32),
            pltpu.VMEM((2, PLANES, LANES), f32),
            pltpu.VMEM((2, PLANES, LANES), f32),
            pltpu.VMEM((2, MIXING + 8, LANES), f32),
            pltpu.VMEM((PLANES, LANES), f32),
            pltpu.SemaphoreType.DMA((6,)),
        ],
        compiler_params=pltpu.CompilerParams(vmem_limit_bytes=24 * 1024 * 1024),
        name="powers",
    )(slab, from_core, from_chip, sides, core_sides, chip_sides, prior_parts)
    inner = sum_over_devices(inner, bands, cols)
    basis_next, triangle = pl.pallas_call(
        finish_kernel,
        out_shape=(
            jax.ShapeDtypeStruct((KPREV, COMPS, 2, ROWS, LANES), f32),
            jax.ShapeDtypeStruct((KPREV, KPREV), f32),
        ),
        in_specs=[VMEM, VMEM, VMEM],
        out_specs=(ANY, VMEM),
        scratch_shapes=[
            pltpu.VMEM((KPREV, COMPS, 2, ROWS, LANES), f32),
            pltpu.SemaphoreType.DMA((COMPS,)),
        ],
        compiler_params=pltpu.CompilerParams(vmem_limit_bytes=24 * 1024 * 1024),
        name="finish",
    )(inner, prior_parts, new_parts)
    basis_next = basis_next.swapaxes(2, 3).reshape(prior_basis.shape)
    return (basis_next, triangle)


def solution(mesh):
    in_specs = (
        P(None, None, None, "band", "col"),
        P(None, None, None, "band", "col"),
        P(None, "band", "col"),
    )
    out_specs = (P(None, None, None, "band", "col"), P())
    return jax.shard_map(
        per_device, mesh=mesh, in_specs=in_specs, out_specs=out_specs, check_vma=False
    )
```
